32 devices in a mesh: row: 8 (over z, core), col: 4 (over y, x).
Axes of the slice: x: 2, y: 2, z: 4, core: 2. Of those that a mesh axis runs over, the one named last changes fastest.
Arguments:
- tokens: bfloat16 [128, 8192], P('row', 'col'), may hold values from -6 to 6
- out_grad: bfloat16 [128, 8192], P('row', 'col'), may hold values from -1.5 to 1.5
- gate_weight: bfloat16 [8192, 16384], P('col', 'row'), may hold values from -0.0625 to 0.0625
- up_weight: bfloat16 [8192, 16384], P('col', 'row'), may hold values from -0.0625 to 0.0625
- down_weight: bfloat16 [16384, 8192], P('row', 'col'), may hold values from -0.046875 to 0.046875
Outputs:
- input_grad: bfloat16 [128, 8192], P('row', 'col')
- gate_weight_grad: bfloat16 [8192, 16384], P('col', 'row')
- up_weight_grad: bfloat16 [8192, 16384], P('col', 'row')
- down_weight_grad: bfloat16 [16384, 8192], P('row', 'col')
The draws below stay inside these ranges and needn't reach their ends.
All inputs are finite; a program needn't handle non-finite values.
Results may differ from the reference program's by a relative error of at most 0.005.
Values may be sent and summed in bfloat16 or wider, within the bound.
A program may use at most 128 MiB of HBM per device.

```python
import jax
import jax.numpy as jnp
from jax import lax

D = 8192
FF = 16384
TOKENS = 128


def block_scale(key, extent, shards, low, top_value):
    gain, own = 1.0, jax.random.fold_in(key, 6)
    for axis_at, parts in shards:
        heights = jnp.exp(jax.random.uniform(jax.random.fold_in(own, axis_at), (parts,), jnp.float32, low / len(shards), top_value / len(shards)))
        gain = gain * jnp.repeat(heights, extent[axis_at] // parts).reshape([-1 if axis == axis_at else 1 for axis in range(len(extent))])
    return gain


def centred(rng, extent, scale, reach, cuts=(), kind=jnp.bfloat16):
    level = block_scale(rng, extent, cuts, -0.22, 0.18) if cuts else 1.0
    values = jax.random.normal(rng, extent, jnp.float32) * scale * level
    return jnp.minimum(jnp.maximum(values, -reach), reach).astype(kind)


def setup_inputs(seed: int = 0) -> dict:
    splits = jax.random.split(jax.random.key(seed), 6)
    return {
        "tokens": centred(splits[0], (TOKENS, D), 1.0, 6.0, ((0, 8), (1, 4))),
        "out_grad": centred(splits[1], (TOKENS, D), 0.25, 1.5, ((0, 8), (1, 4))),
        "gate_weight": centred(splits[2], (D, FF), D ** -0.5, 0.0625, ((0, 4), (1, 8))),
        "up_weight": centred(splits[3], (D, FF), D ** -0.5, 0.0625, ((0, 4), (1, 8))),
        "down_weight": centred(splits[4], (FF, D), FF ** -0.5, 0.046875, ((0, 8), (1, 4))),
    }


def reference(tokens, out_grad, gate_weight, up_weight, down_weight):
    gate = jnp.dot(tokens, gate_weight, preferred_element_type=jnp.float32)
    up = jnp.dot(tokens, up_weight, preferred_element_type=jnp.float32)
    hidden_grad = lax.dot_general(out_grad, down_weight, (((1,), (1,)), ((), ())), preferred_element_type=jnp.float32)
    sig = jax.nn.sigmoid(gate)
    act = gate * sig
    hidden = (act * up).astype(jnp.bfloat16)
    gate_grad = (hidden_grad * up * sig * (1.0 + gate * (1.0 - sig))).astype(jnp.bfloat16)
    up_grad = (hidden_grad * act).astype(jnp.bfloat16)
    contract_rows = (((0,), (0,)), ((), ()))
    gate_weight_grad = lax.dot_general(tokens, gate_grad, contract_rows, preferred_element_type=jnp.float32).astype(jnp.bfloat16)
    up_weight_grad = lax.dot_general(tokens, up_grad, contract_rows, preferred_element_type=jnp.float32).astype(jnp.bfloat16)
    down_weight_grad = lax.dot_general(hidden, out_grad, contract_rows, preferred_element_type=jnp.float32).astype(jnp.bfloat16)
    contract_cols = (((1,), (1,)), ((), ()))
    input_grad = lax.dot_general(gate_grad, gate_weight, contract_cols, preferred_element_type=jnp.float32)
    input_grad = input_grad + lax.dot_general(up_grad, up_weight, contract_cols, preferred_element_type=jnp.float32)
    return (input_grad.astype(jnp.bfloat16), gate_weight_grad, up_weight_grad, down_weight_grad)
```

```python
import functools

import jax
import jax.numpy as jnp
from jax import lax
from jax.experimental import pallas as pl
from jax.experimental.pallas import tpu as pltpu
from jax.sharding import PartitionSpec as P

F32, BF16 = jnp.float32, jnp.bfloat16
MESH = pl.DeviceIdType.MESH
NN = (((1,), (0,)), ((), ()))
NT = (((1,), (1,)), ((), ()))
TN = (((0,), (0,)), ((), ()))


def mm(a, b, dims):
    return lax.dot_general(a, b, dims, preferred_element_type=F32)


def xor(a, b, n):
    out, bit = 0, 1
    while bit < n:
        out = out + lax.rem(a // bit + (b // bit) % 2, 2) * bit
        bit *= 2
    return out


def layer_kernel(
    nrow, ncol,
    tok_ref, og_ref, gw_hbm, uw_hbm, dw_hbm,
    rows_hbm, grads_hbm, res_hbm, ig_ref,
    gw, uw, dw, rows, grads, part, wide, inbox, res, tot, sib, pair, pbox,
    w_sem, out_sem, g_send, g_recv, f_send, f_recv,
    rs_send, rs_recv, ag_send, ag_recv, s_send, s_recv, p_send, p_recv,
):
    nz = nrow // 2
    nc, d_loc, cw = gw.shape
    tb = tok_ref.shape[0]
    tc = rows.shape[0] // ncol
    r, me = lax.axis_index("row"), lax.axis_index("col")
    z, core = r // 2, lax.rem(r, 2)
    sibling = z * 2 + 1 - core

    def block(i, n):
        return pl.ds(pl.multiple_of(i * n, n), n)

    barrier = pltpu.get_barrier_semaphore()
    pl.semaphore_signal(barrier, inc=1, device_id={"row": sibling}, device_id_type=MESH)
    for k in range(1, nz):
        pl.semaphore_signal(barrier, inc=1, device_id={"row": xor(z, k, nz) * 2 + core}, device_id_type=MESH)
    for k in range(1, ncol):
        pl.semaphore_signal(barrier, inc=1, device_id={"col": xor(me, k, ncol)}, device_id_type=MESH)

    def weight_copy(i, c):
        cols = block(c, cw)
        src = dw_hbm.at[cols, :] if i == 2 else (gw_hbm, uw_hbm)[i].at[:, cols]
        return pltpu.make_async_copy(src, (gw, uw, dw)[i].at[c], w_sem.at[i, c])

    for c in range(nc):
        weight_copy(0, c).start()
        weight_copy(1, c).start()
    for c in range(nc):
        weight_copy(2, c).start()
    rows[block(r, tb), :] = tok_ref[...]
    grads[block(r, tb), :] = og_ref[...]
    pl.semaphore_wait(barrier, nz + ncol - 1)

    def gather_copy(a, k):
        buf = (rows, grads)[a]
        mine = buf.at[block(r, tb), :]
        to = sibling if k == 0 else xor(z, k, nz) * 2 + core
        return pltpu.make_async_remote_copy(
            mine, mine, g_send.at[a, k], g_recv.at[a, k], device_id={"row": to}, device_id_type=MESH
        )

    def forward_copy(a, k):
        buf = (rows, grads)[a]
        got = buf.at[block(xor(z, k, nz) * 2 + core, tb), :]
        return pltpu.make_async_remote_copy(
            got, got, f_send.at[a, k - 1], f_recv.at[a, k - 1], device_id={"row": sibling}, device_id_type=MESH
        )

    def finish_gather(a):
        for k in range(1, nz):
            gather_copy(a, k).wait_recv()
            forward_copy(a, k).start()
        gather_copy(a, 0).wait_recv()
        for k in range(1, nz):
            forward_copy(a, k).wait_recv()

    for a in range(2):
        for k in range(nz):
            gather_copy(a, k).start()

    def part_copy(c, kind, k):
        to = xor(me, k, ncol)
        which = pl.ds(0, 2) if kind == 0 else pl.ds(2, 1)
        return pltpu.make_async_remote_copy(
            part.at[c, which, block(to, tc), :], inbox.at[c, k - 1, which],
            rs_send.at[kind, c, k - 1], rs_recv.at[kind, c, k - 1],
            device_id={"col": to}, device_id_type=MESH,
        )

    out_rows = pltpu.make_async_copy(rows, rows_hbm, out_sem.at[0])
    out_grads = pltpu.make_async_copy(grads, grads_hbm, out_sem.at[1])
    out_res = pltpu.make_async_copy(res, res_hbm, out_sem.at[2])

    def keep(c, i, product):
        part[c, i] = product.astype(BF16)
        wide[c, i] = product

    finish_gather(0)
    out_rows.start()

    @pl.loop(0, nc)
    def _(c):
        for i, w in ((0, gw), (1, uw)):
            weight_copy(i, c).wait()
            keep(c, i, mm(rows[...], w[c], NN))
        for k in range(1, ncol):
            part_copy(c, 0, k).start()

    finish_gather(1)
    out_grads.start()

    @pl.loop(0, nc)
    def _(c):
        weight_copy(2, c).wait()
        keep(c, 2, mm(grads[...], dw[c], NT))
        for k in range(1, ncol):
            part_copy(c, 1, k).start()

    def res_copy(c, k):
        mine = res.at[c, :, block(me, tc), :]
        return pltpu.make_async_remote_copy(
            mine, mine, ag_send.at[c, k - 1], ag_recv.at[c, k - 1],
            device_id={"col": xor(me, k, ncol)}, device_id_type=MESH,
        )

    @pl.loop(0, nc)
    def _(c):
        own = block(me, tc)
        sums = [wide[c, i, own, :] for i in range(3)]
        for k in range(1, ncol):
            part_copy(c, 0, k).wait_recv()
            part_copy(c, 1, k).wait_recv()
            sums = [sums[i] + inbox[c, k - 1, i].astype(F32) for i in range(3)]
        gate, up, hidden_grad = sums
        sig = 1.0 / (1.0 + jnp.exp(-gate))
        act = gate * sig
        res[c, 0, own, :] = (act * up).astype(BF16)
        res[c, 1, own, :] = (hidden_grad * up * sig * (1.0 + gate * (1.0 - sig))).astype(BF16)
        res[c, 2, own, :] = (hidden_grad * act).astype(BF16)
        for k in range(1, ncol):
            res_copy(c, k).start()

    td = min(512, d_loc)
    tot[...] = jnp.zeros_like(tot)

    @pl.loop(0, nc)
    def _(c):
        for k in range(1, ncol):
            res_copy(c, k).wait_recv()
        for j in range(d_loc // td):
            cut = pl.ds(j * td, td)
            tot[:, cut] += mm(res[c, 1], gw[c, cut, :], NT) + mm(res[c, 2], uw[c, cut, :], NT)

    out_res.start()

    def sib_copy(k):
        return pltpu.make_async_remote_copy(
            tot.at[block(2 * k + 1 - core, tb), :], sib.at[k], s_send.at[k], s_recv.at[k],
            device_id={"row": sibling}, device_id_type=MESH,
        )

    def pair_copy(k):
        to = xor(z, k, nz)
        return pltpu.make_async_remote_copy(
            pair.at[to], pbox.at[k - 1], p_send.at[k - 1], p_recv.at[k - 1],
            device_id={"row": to * 2 + core}, device_id_type=MESH,
        )

    for k in range(nz):
        sib_copy(k).start()
    for k in range(nz):
        sib_copy(k).wait_recv()
    for k in range(nz):
        pair[k] = (tot[block(2 * k + core, tb), :] + sib[k]).astype(BF16)
    for k in range(1, nz):
        pair_copy(k).start()
    total = tot[block(r, tb), :] + sib[z]
    for k in range(1, nz):
        pair_copy(k).wait_recv()
        total = total + pbox[k - 1].astype(F32)
    ig_ref[...] = total.astype(BF16)

    for a in range(2):
        for k in range(nz):
            gather_copy(a, k).wait_send()
        for k in range(1, nz):
            forward_copy(a, k).wait_send()
    for k in range(1, ncol):
        @pl.loop(0, nc)
        def _(c):
            part_copy(c, 0, k).wait_send()
            part_copy(c, 1, k).wait_send()
            res_copy(c, k).wait_send()
    for k in range(nz):
        sib_copy(k).wait_send()
    for k in range(1, nz):
        pair_copy(k).wait_send()
    out_rows.wait()
    out_grads.wait()
    out_res.wait()


def layer(nrow, ncol, tokens, out_grad, gate_weight, up_weight, down_weight):
    tb, d_loc = tokens.shape
    ff = gate_weight.shape[1]
    t = tb * nrow
    cw = min(512, ff)
    nc, nz, tc = ff // cw, nrow // 2, t // ncol
    vmem = pl.BlockSpec(memory_space=pltpu.VMEM)
    hbm = pl.BlockSpec(memory_space=pl.ANY)
    dma = pltpu.SemaphoreType.DMA
    return pl.pallas_call(
        functools.partial(layer_kernel, nrow, ncol),
        out_shape=(
            jax.ShapeDtypeStruct((t, d_loc), BF16),
            jax.ShapeDtypeStruct((t, d_loc), BF16),
            jax.ShapeDtypeStruct((nc, 3, t, cw), BF16),
            jax.ShapeDtypeStruct((tb, d_loc), BF16),
        ),
        in_specs=[vmem, vmem, hbm, hbm, hbm],
        out_specs=(hbm, hbm, hbm, vmem),
        scratch_shapes=[
            pltpu.VMEM((nc, d_loc, cw), BF16),
            pltpu.VMEM((nc, d_loc, cw), BF16),
            pltpu.VMEM((nc, cw, d_loc), BF16),
            pltpu.VMEM((t, d_loc), BF16),
            pltpu.VMEM((t, d_loc), BF16),
            pltpu.VMEM((nc, 3, t, cw), BF16),
            pltpu.VMEM((nc, 3, t, cw), F32),
            pltpu.VMEM((nc, ncol - 1, 3, tc, cw), BF16),
            pltpu.VMEM((nc, 3, t, cw), BF16),
            pltpu.VMEM((t, d_loc), F32),
            pltpu.VMEM((nz, tb, d_loc), F32),
            pltpu.VMEM((nz, tb, d_loc), BF16),
            pltpu.VMEM((nz - 1, tb, d_loc), BF16),
            dma((3, nc)), dma((3,)),
            dma((2, nz)), dma((2, nz)), dma((2, nz - 1)), dma((2, nz - 1)),
            dma((2, nc, ncol - 1)), dma((2, nc, ncol - 1)),
            dma((nc, ncol - 1)), dma((nc, ncol - 1)),
            dma((nz,)), dma((nz,)), dma((nz - 1,)), dma((nz - 1,)),
        ],
        compiler_params=pltpu.CompilerParams(
            collective_id=0, has_side_effects=True, vmem_limit_bytes=48 * 1024 * 1024
        ),
        cost_estimate=pl.CostEstimate(
            flops=10 * t * d_loc * ff, bytes_accessed=6 * d_loc * ff, transcendentals=t * ff
        ),
    )(tokens, out_grad, gate_weight, up_weight, down_weight)


def grads_kernel(rows_ref, grads_ref, res_ref, hid_ref, gwg_ref, uwg_ref, dwg_ref):
    nc, _, _, cw = res_ref.shape
    for c in range(nc):
        cols = pl.ds(c * cw, cw)
        gwg_ref[:, cols] = mm(rows_ref[...], res_ref[c, 1], TN).astype(BF16)
        uwg_ref[:, cols] = mm(rows_ref[...], res_ref[c, 2], TN).astype(BF16)
    d_loc = grads_ref.shape[1]
    step = min(512, d_loc)
    for j in range(d_loc // step):
        cols = pl.ds(j * step, step)
        dwg_ref[:, cols] = mm(hid_ref[0, 0], grads_ref[:, cols], TN).astype(BF16)


def weight_grads(rows, grads, res):
    t, d_loc = rows.shape
    nc, _, _, cw = res.shape
    ff = nc * cw
    tile = min(256, cw)
    steps = ff // tile
    td = d_loc // steps
    per = cw // tile
    return pl.pallas_call(
        grads_kernel,
        grid=(steps,),
        out_shape=(
            jax.ShapeDtypeStruct((d_loc, ff), BF16),
            jax.ShapeDtypeStruct((d_loc, ff), BF16),
            jax.ShapeDtypeStruct((ff, d_loc), BF16),
        ),
        in_specs=[
            pl.BlockSpec((t, td), lambda i: (0, i)),
            pl.BlockSpec((t, d_loc), lambda i: (0, 0)),
            pl.BlockSpec((nc, 3, t, cw), lambda i: (0, 0, 0, 0)),
            pl.BlockSpec((1, 1, t, tile), lambda i: (i // per, 0, 0, i % per)),
        ],
        out_specs=(
            pl.BlockSpec((td, ff), lambda i: (i, 0)),
            pl.BlockSpec((td, ff), lambda i: (i, 0)),
            pl.BlockSpec((tile, d_loc), lambda i: (i, 0)),
        ),
        compiler_params=pltpu.CompilerParams(vmem_limit_bytes=32 * 1024 * 1024),
        cost_estimate=pl.CostEstimate(
            flops=6 * t * d_loc * ff, bytes_accessed=6 * d_loc * ff, transcendentals=0
        ),
    )(rows, grads, res, res)


def solution(mesh):
    nrow, ncol = mesh.shape["row"], mesh.shape["col"]

    def body(tokens, out_grad, gate_weight, up_weight, down_weight):
        rows, grads, res, input_grad = layer(
            nrow, ncol, tokens, out_grad, gate_weight, up_weight, down_weight
        )
        return (input_grad, *weight_grads(rows, grads, res))

    return jax.shard_map(
        body,
        mesh=mesh,
        in_specs=(
            P("row", "col"),
            P("row", "col"),
            P("col", "row"),
            P("col", "row"),
            P("row", "col"),
        ),
        out_specs=(P("row", "col"), P("col", "row"), P("col", "row"), P("row", "col")),
        check_vma=False,
    )
```

```python
import functools

import jax
import jax.numpy as jnp
from jax import lax
from jax.experimental import pallas as pl
from jax.experimental.pallas import tpu as pltpu
from jax.sharding import PartitionSpec as P

F32, BF16 = jnp.float32, jnp.bfloat16
MESH = pl.DeviceIdType.MESH
NN = (((1,), (0,)), ((), ()))
NT = (((1,), (1,)), ((), ()))
TN = (((0,), (0,)), ((), ()))


def mm(a, b, dims):
    return lax.dot_general(a, b, dims, preferred_element_type=F32)


def xor(a, b, n):
    out, bit = 0, 1
    while bit < n:
        out = out + lax.rem(a // bit + (b // bit) % 2, 2) * bit
        bit *= 2
    return out


def layer_kernel(
    nrow, ncol,
    tok_ref, og_ref, gw_hbm, uw_hbm, dw_hbm,
    rows_hbm, grads_hbm, res_hbm, own_ref, *more,
):
    nz = nrow // 2
    pair_refs = more[: nz - 1]
    (
        gw, uw, dw, rows, grads, part, wide, inbox, res, tot, sib,
        in_sem, w_sem, out_sem, g_send, g_recv, f_send, f_recv,
        rs_send, rs_recv, ag_send, ag_recv, fw_send, fw_recv, s_send, s_recv,
    ) = more[nz - 1 :]
    nc, d_loc, cw = gw.shape
    tb = tok_ref.shape[0]
    tc = rows.shape[0] // ncol
    r, me = lax.axis_index("row"), lax.axis_index("col")
    z, core = r // 2, lax.rem(r, 2)
    sibling = z * 2 + 1 - core

    def block(i, n):
        return pl.ds(pl.multiple_of(i * n, n), n)

    barrier = pltpu.get_barrier_semaphore()
    pl.semaphore_signal(barrier, inc=1, device_id={"row": sibling}, device_id_type=MESH)
    for k in range(1, nz):
        pl.semaphore_signal(barrier, inc=1, device_id={"row": xor(z, k, nz) * 2 + core}, device_id_type=MESH)
    for k in range(1, ncol):
        pl.semaphore_signal(barrier, inc=1, device_id={"col": xor(me, k, ncol)}, device_id_type=MESH)

    def weight_copy(i, c):
        cols = block(c, cw)
        src = dw_hbm.at[cols, :] if i == 2 else (gw_hbm, uw_hbm)[i].at[:, cols]
        return pltpu.make_async_copy(src, (gw, uw, dw)[i].at[c], w_sem.at[i, c])

    own_tok = pltpu.make_async_copy(tok_ref, rows.at[block(r, tb), :], in_sem.at[0])
    own_og = pltpu.make_async_copy(og_ref, grads.at[block(r, tb), :], in_sem.at[1])
    own_tok.start()
    own_og.start()
    for c in range(nc):
        weight_copy(0, c).start()
        weight_copy(1, c).start()
    for c in range(nc):
        weight_copy(2, c).start()
    own_tok.wait()
    own_og.wait()
    pl.semaphore_wait(barrier, nz + ncol - 1)

    def gather_copy(a, k):
        buf = (rows, grads)[a]
        mine = buf.at[block(r, tb), :]
        to = sibling if k == 0 else xor(z, k, nz) * 2 + core
        return pltpu.make_async_remote_copy(
            mine, mine, g_send.at[a, k], g_recv.at[a, k], device_id={"row": to}, device_id_type=MESH
        )

    def forward_copy(a, k):
        buf = (rows, grads)[a]
        got = buf.at[block(xor(z, k, nz) * 2 + core, tb), :]
        return pltpu.make_async_remote_copy(
            got, got, f_send.at[a, k - 1], f_recv.at[a, k - 1], device_id={"row": sibling}, device_id_type=MESH
        )

    def finish_gather(a):
        for k in range(1, nz):
            gather_copy(a, k).wait_recv()
            forward_copy(a, k).start()
        if a == 0:
            for k in range(nz):
                gather_copy(1, k).start()
        gather_copy(a, 0).wait_recv()
        for k in range(1, nz):
            forward_copy(a, k).wait_recv()

    for k in range(nz):
        gather_copy(0, k).start()

    def part_copy(c, kind, k):
        to = xor(me, k, ncol)
        which = pl.ds(0, 2) if kind == 0 else pl.ds(2, 1)
        return pltpu.make_async_remote_copy(
            part.at[c, which, block(to, tc), :], inbox.at[c, k - 1, which],
            rs_send.at[kind, c, k - 1], rs_recv.at[kind, c, k - 1],
            device_id={"col": to}, device_id_type=MESH,
        )

    out_rows = pltpu.make_async_copy(rows, rows_hbm, out_sem.at[0])
    out_grads = pltpu.make_async_copy(grads, grads_hbm, out_sem.at[1])
    out_res = pltpu.make_async_copy(res, res_hbm, out_sem.at[2])

    def keep(c, i, product):
        part[c, i] = product.astype(BF16)
        wide[c, i] = product

    finish_gather(0)
    out_rows.start()

    @pl.loop(0, nc)
    def _(c):
        for i, w in ((0, gw), (1, uw)):
            weight_copy(i, c).wait()
            keep(c, i, mm(rows[...], w[c], NN))
        for k in range(1, ncol):
            part_copy(c, 0, k).start()

    finish_gather(1)
    out_grads.start()

    @pl.loop(0, nc)
    def _(c):
        weight_copy(2, c).wait()
        keep(c, 2, mm(grads[...], dw[c], NT))
        for k in range(1, ncol):
            part_copy(c, 1, k).start()

    def res_copy(c, k):
        mine = res.at[c, :, block(me, tc), :]
        return pltpu.make_async_remote_copy(
            mine, mine, ag_send.at[c, k - 1], ag_recv.at[c, k - 1],
            device_id={"col": xor(me, k, ncol)}, device_id_type=MESH,
        )

    relayed = ncol == 4 and tc % 32 == 0
    direct = (1, 2) if relayed else tuple(range(1, ncol))

    def relay_copy(c, k):
        half = pl.ds(pl.multiple_of(xor(me, k, ncol) * tc + (k - 1) * (tc // 2), tc // 2), tc // 2)
        got = res.at[c, :, half, :]
        return pltpu.make_async_remote_copy(
            got, got, fw_send.at[c, k - 1], fw_recv.at[c, k - 1],
            device_id={"col": xor(me, 3 - k, ncol)}, device_id_type=MESH,
        )

    def arrive(c):
        for k in direct:
            res_copy(c, k).wait_recv()
            if relayed:
                relay_copy(c, k).start()

    @pl.loop(0, nc)
    def _(c):
        own = block(me, tc)
        sums = [wide[c, i, own, :] for i in range(3)]
        for k in range(1, ncol):
            part_copy(c, 0, k).wait_recv()
            part_copy(c, 1, k).wait_recv()
            sums = [sums[i] + inbox[c, k - 1, i].astype(F32) for i in range(3)]
        gate, up, hidden_grad = sums
        sig = 1.0 / (1.0 + jnp.exp(-gate))
        act = gate * sig
        res[c, 0, own, :] = (act * up).astype(BF16)
        res[c, 1, own, :] = (hidden_grad * up * sig * (1.0 + gate * (1.0 - sig))).astype(BF16)
        res[c, 2, own, :] = (hidden_grad * act).astype(BF16)
        for k in direct:
            res_copy(c, k).start()

    td = min(512, d_loc)
    tot[...] = jnp.zeros_like(tot)

    arrive(0)

    @pl.loop(0, nc)
    def _(c):
        @pl.when(c + 1 < nc)
        def _():
            arrive(c + 1)

        if relayed:
            for k in (1, 2):
                relay_copy(c, k).wait_recv()
        for j in range(d_loc // td):
            cut = pl.ds(j * td, td)
            tot[:, cut] += mm(res[c, 1], gw[c, cut, :], NT) + mm(res[c, 2], uw[c, cut, :], NT)

    out_res.start()

    def sib_copy(k):
        return pltpu.make_async_remote_copy(
            tot.at[block(2 * k + 1 - core, tb), :], sib.at[k], s_send.at[k], s_recv.at[k],
            device_id={"row": sibling}, device_id_type=MESH,
        )

    for k in range(nz):
        sib_copy(k).start()
    for k in range(nz):
        sib_copy(k).wait_recv()
    own_ref[...] = tot[block(r, tb), :] + sib[z]
    for k in range(1, nz):
        to = xor(z, k, nz)
        pair_refs[k - 1][...] = (tot[block(2 * to + core, tb), :] + sib[to]).astype(BF16)

    for a in range(2):
        for k in range(nz):
            gather_copy(a, k).wait_send()
        for k in range(1, nz):
            forward_copy(a, k).wait_send()
    for k in range(1, ncol):
        @pl.loop(0, nc)
        def _(c):
            part_copy(c, 0, k).wait_send()
            part_copy(c, 1, k).wait_send()
            if k in direct:
                res_copy(c, k).wait_send()
            if relayed and k < 3:
                relay_copy(c, k).wait_send()
    for k in range(nz):
        sib_copy(k).wait_send()
    out_rows.wait()
    out_grads.wait()
    out_res.wait()


def layer(nrow, ncol, tokens, out_grad, gate_weight, up_weight, down_weight):
    tb, d_loc = tokens.shape
    ff = gate_weight.shape[1]
    t = tb * nrow
    cw = min(512, ff)
    nc, nz, tc = ff // cw, nrow // 2, t // ncol
    vmem = pl.BlockSpec(memory_space=pltpu.VMEM)
    hbm = pl.BlockSpec(memory_space=pl.ANY)
    dma = pltpu.SemaphoreType.DMA
    return pl.pallas_call(
        functools.partial(layer_kernel, nrow, ncol),
        out_shape=(
            jax.ShapeDtypeStruct((t, d_loc), BF16),
            jax.ShapeDtypeStruct((t, d_loc), BF16),
            jax.ShapeDtypeStruct((nc, 3, t, cw), BF16),
            jax.ShapeDtypeStruct((tb, d_loc), F32),
            *[jax.ShapeDtypeStruct((tb, d_loc), BF16)] * (nz - 1),
        ),
        in_specs=[pl.BlockSpec(memory_space=pltpu.HBM)] * 5,
        out_specs=(hbm, hbm, hbm) + (vmem,) * nz,
        scratch_shapes=[
            pltpu.VMEM((nc, d_loc, cw), BF16),
            pltpu.VMEM((nc, d_loc, cw), BF16),
            pltpu.VMEM((nc, cw, d_loc), BF16),
            pltpu.VMEM((t, d_loc), BF16),
            pltpu.VMEM((t, d_loc), BF16),
            pltpu.VMEM((nc, 3, t, cw), BF16),
            pltpu.VMEM((nc, 3, t, cw), F32),
            pltpu.VMEM((nc, ncol - 1, 3, tc, cw), BF16),
            pltpu.VMEM((nc, 3, t, cw), BF16),
            pltpu.VMEM((t, d_loc), F32),
            pltpu.VMEM((nz, tb, d_loc), F32),
            dma((2,)), dma((3, nc)), dma((3,)),
            dma((2, nz)), dma((2, nz)), dma((2, nz - 1)), dma((2, nz - 1)),
            dma((2, nc, ncol - 1)), dma((2, nc, ncol - 1)),
            dma((nc, ncol - 1)), dma((nc, ncol - 1)), dma((nc, 2)), dma((nc, 2)),
            dma((nz,)), dma((nz,)),
        ],
        compiler_params=pltpu.CompilerParams(
            collective_id=0, has_side_effects=True, vmem_limit_bytes=48 * 1024 * 1024
        ),
        cost_estimate=pl.CostEstimate(
            flops=10 * t * d_loc * ff, bytes_accessed=6 * d_loc * ff, transcendentals=t * ff
        ),
    )(tokens, out_grad, gate_weight, up_weight, down_weight)


def grads_kernel(rows_ref, grads_ref, res_ref, hid_ref, gwg_ref, uwg_ref, dwg_ref):
    nc, _, _, cw = res_ref.shape
    for c in range(nc):
        cols = pl.ds(c * cw, cw)
        gwg_ref[:, cols] = mm(rows_ref[...], res_ref[c, 1], TN).astype(BF16)
        uwg_ref[:, cols] = mm(rows_ref[...], res_ref[c, 2], TN).astype(BF16)
    d_loc = grads_ref.shape[1]
    step = min(512, d_loc)
    for j in range(d_loc // step):
        cols = pl.ds(j * step, step)
        dwg_ref[:, cols] = mm(hid_ref[0, 0], grads_ref[:, cols], TN).astype(BF16)


def weight_grads(rows, grads, res):
    t, d_loc = rows.shape
    nc, _, _, cw = res.shape
    ff = nc * cw
    tile = min(256, cw)
    steps = ff // tile
    td = d_loc // steps
    per = cw // tile
    return pl.pallas_call(
        grads_kernel,
        grid=(steps,),
        out_shape=(
            jax.ShapeDtypeStruct((d_loc, ff), BF16),
            jax.ShapeDtypeStruct((d_loc, ff), BF16),
            jax.ShapeDtypeStruct((ff, d_loc), BF16),
        ),
        in_specs=[
            pl.BlockSpec((t, td), lambda i: (0, i)),
            pl.BlockSpec((t, d_loc), lambda i: (0, 0)),
            pl.BlockSpec((nc, 3, t, cw), lambda i: (0, 0, 0, 0)),
            pl.BlockSpec((1, 1, t, tile), lambda i: (i // per, 0, 0, i % per)),
        ],
        out_specs=(
            pl.BlockSpec((td, ff), lambda i: (i, 0)),
            pl.BlockSpec((td, ff), lambda i: (i, 0)),
            pl.BlockSpec((tile, d_loc), lambda i: (i, 0)),
        ),
        compiler_params=pltpu.CompilerParams(vmem_limit_bytes=32 * 1024 * 1024),
        cost_estimate=pl.CostEstimate(
            flops=6 * t * d_loc * ff, bytes_accessed=6 * d_loc * ff, transcendentals=0
        ),
    )(rows, grads, res, res)


def solution(mesh):
    nrow, ncol = mesh.shape["row"], mesh.shape["col"]

    def body(tokens, out_grad, gate_weight, up_weight, down_weight):
        rows, grads, res, total, *pairs = layer(
            nrow, ncol, tokens, out_grad, gate_weight, up_weight, down_weight
        )
        got = [
            lax.ppermute(p, "row", [(r, (r // 2 ^ k) * 2 + r % 2) for r in range(nrow)])
            for k, p in enumerate(pairs, 1)
        ]
        weights = weight_grads(rows, grads, res)
        for p in got:
            total = total + p.astype(F32)
        return (total.astype(BF16), *weights)

    return jax.shard_map(
        body,
        mesh=mesh,
        in_specs=(
            P("row", "col"),
            P("row", "col"),
            P("col", "row"),
            P("col", "row"),
            P("row", "col"),
        ),
        out_specs=(P("row", "col"), P("col", "row"), P("col", "row"), P("row", "col")),
        check_vma=False,
    )
```
